32 devices in a mesh: groups: 2 (over y), chan: 4 (over z), space: 4 (over x, core).
Axes of the slice: x: 2, y: 2, z: 4, core: 2. Of those that a mesh axis runs over, the one named last changes fastest.
Arguments:
- volume: bfloat16 [2048, 16, 512], P(('groups', 'chan'), 'space'), parts along dimension 0, may hold values from -6 to 6
- out_grad: bfloat16 [2048, 16, 512], P(('groups', 'chan'), 'space'), parts along dimension 0, may hold values from -6 to 6
- weight_in: bfloat16 [1024, 1024], P('chan'), may hold values from -0.1875 to 0.1875
- weight_out: bfloat16 [1024, 1024], P('chan'), may hold values from -0.1875 to 0.1875
- filter_taps: float32 [1024, 27], P('chan'), may hold values from -1.25 to 1.25
- filter_bias: float32 [1024], P('chan'), may hold values from -3 to 3
Outputs:
- block_out: bfloat16 [2048, 16, 512], P(('groups', 'chan'), 'space'), parts along dimension 0
- volume_grad: bfloat16 [2048, 16, 512], P(('groups', 'chan'), 'space'), parts along dimension 0
The draws below stay inside these ranges and needn't reach their ends.
There are 2 independent parts, one for each index of `groups`. The reference program is written for one: setup_inputs(seed, part) draws one part's arguments, and reference() takes and returns one part's arrays. A program takes and returns all parts, laid end to end along the dimension named above; an argument that names none is the same for every part. Nothing has to cross between parts.
All inputs are finite; a program needn't handle non-finite values.
Results may differ from the reference program's by a relative error of at most 0.0085.
Values may be sent and summed in bfloat16 or wider, within the bound.
A program may use at most 64 MiB of HBM per device.

```python
import jax
import jax.numpy as jnp
from jax import lax

C = 1024
TAPS = 27
CX = 32
CY = 16
NZ = 16
PLANE = 512


def shard_levels(rng, dims, split, low, largest):
    level, own = 1.0, jax.random.fold_in(rng, 6)
    for dim, parts in split:
        heights = jnp.exp(jax.random.uniform(jax.random.fold_in(own, dim), (parts,), jnp.float32, low / len(split), largest / len(split)))
        level = level * jnp.repeat(heights, dims[dim] // parts).reshape([-1 if axis == dim else 1 for axis in range(len(dims))])
    return level


def gaussian(own_key, dims, width, limit, cuts=(), dtype=jnp.bfloat16):
    entries = width * jax.random.normal(own_key, dims, jnp.float32)
    if cuts:
        entries = entries * shard_levels(own_key, dims, cuts, -0.22, 0.18)
    return jnp.clip(entries, -limit, limit).astype(dtype)


def setup_inputs(seed: int = 0, part: int = 0) -> dict:
    streams_of = jax.random.split(jax.random.key(seed), 7)
    part_splits = jax.random.split(jax.random.fold_in(streams_of[6], part), 7)
    return {
        "volume": gaussian(part_splits[0], (C, NZ, PLANE), 1.0, 6.0, ((0, 4), (1, 4))),
        "out_grad": gaussian(part_splits[1], (C, NZ, PLANE), 1.0, 6.0, ((0, 4), (1, 4))),
        "weight_in": gaussian(streams_of[2], (C, C), C ** -0.5, 0.1875, ((0, 4),)),
        "weight_out": gaussian(streams_of[3], (C, C), C ** -0.5, 0.1875, ((0, 4),)),
        "filter_taps": gaussian(streams_of[4], (C, TAPS), TAPS ** -0.5, 1.25, ((0, 4),), jnp.float32),
        "filter_bias": gaussian(streams_of[5], (C,), 0.5, 3.0, ((0, 4),), jnp.float32),
    }


root_half = 0.7071067811865476
inv_root_two_pi = 0.3989422804014327


def gelu_value(field):
    return 0.5 * field * (1.0 + lax.erf(field * root_half))


def gelu_slope(field):
    return 0.5 * (1.0 + lax.erf(field * root_half)) + field * jnp.exp(-0.5 * field * field) * inv_root_two_pi


def core(padded, filter_taps, direction):
    extent_z = padded.shape[1] - 2
    extent_y = padded.shape[2] - 2
    extent_x = padded.shape[3] - 2
    summed = jnp.zeros((padded.shape[0], extent_z, extent_y, extent_x), jnp.float32)
    for shift_z in range(3):
        for shift_y in range(3):
            for shift_x in range(3):
                tap_index = (shift_z * 3 + shift_y) * 3 + shift_x
                begin_z = 1 + direction * (shift_z - 1)
                begin_y = 1 + direction * (shift_y - 1)
                begin_x = 1 + direction * (shift_x - 1)
                window = padded[:, begin_z:begin_z + extent_z, begin_y:begin_y + extent_y, begin_x:begin_x + extent_x]
                summed = summed + filter_taps[:, tap_index][:, None, None, None] * window
    return summed


def reference(volume, out_grad, weight_in, weight_out, filter_taps, filter_bias):
    channels = volume.shape[0]
    slab_shape = volume.shape
    grid_shape = (channels, volume.shape[1], CY, CX)
    pads = ((0, 0), (1, 1), (1, 1), (1, 1))
    flat_in = volume.reshape(channels, -1)
    hidden = jnp.dot(weight_in, flat_in, preferred_element_type=jnp.float32).astype(jnp.bfloat16)
    padded = jnp.pad(hidden.astype(jnp.float32).reshape(grid_shape), pads)
    mixed = core(padded, filter_taps, 1) + filter_bias[:, None, None, None]
    active = gelu_value(mixed).astype(jnp.bfloat16)
    block_out = (flat_in.astype(jnp.float32) + jnp.dot(weight_out, active.reshape(channels, -1), preferred_element_type=jnp.float32)).astype(jnp.bfloat16).reshape(slab_shape)
    flat_grad = out_grad.reshape(channels, -1)
    act_grad = jnp.dot(weight_out.T, flat_grad, preferred_element_type=jnp.float32).astype(jnp.bfloat16)
    mix_grad = (act_grad.astype(jnp.float32).reshape(grid_shape) * gelu_slope(mixed)).astype(jnp.bfloat16)
    padded_grad = jnp.pad(mix_grad.astype(jnp.float32), pads)
    hid_grad = core(padded_grad, filter_taps, -1).astype(jnp.bfloat16)
    volume_grad = (flat_grad.astype(jnp.float32) + jnp.dot(weight_in.T, hid_grad.reshape(channels, -1), preferred_element_type=jnp.float32)).astype(jnp.bfloat16).reshape(slab_shape)
    return block_out, volume_grad
```

```python
import functools

import jax
import jax.numpy as jnp
from jax import lax
from jax.experimental import pallas as pl
from jax.experimental.pallas import tpu as pltpu
from jax.sharding import PartitionSpec as P

CX = 32
CY = 16


root_half = 0.7071067811865476
inv_root_two_pi = 0.3989422804014327


def with_halo(block, sides, width):
    for axis, dim in sides:
        count = lax.axis_size(axis)
        forward = [(i, i + 1) for i in range(count - 1)]
        backward = [(target, source) for source, target in forward]
        low = lax.ppermute(
            lax.slice_in_dim(block, block.shape[dim] - width, None, axis=dim), axis, forward
        )
        high = lax.ppermute(lax.slice_in_dim(block, 0, width, axis=dim), axis, backward)
        block = jnp.concatenate([low, block, high], axis=dim)
    return block


def gelu_value(field):
    return 0.5 * field * (1.0 + lax.erf(field * root_half))


def gelu_slope(field):
    return (
        0.5 * (1.0 + lax.erf(field * root_half))
        + field * jnp.exp(-0.5 * field * field) * inv_root_two_pi
    )


def core(padded, filter_taps, direction):
    extent_z = padded.shape[1] - 2
    extent_y = padded.shape[2] - 2
    extent_x = padded.shape[3] - 2
    summed = jnp.zeros((padded.shape[0], extent_z, extent_y, extent_x), jnp.float32)
    for shift_z in range(3):
        for shift_y in range(3):
            for shift_x in range(3):
                tap_index = (shift_z * 3 + shift_y) * 3 + shift_x
                begin_z = 1 + direction * (shift_z - 1)
                begin_y = 1 + direction * (shift_y - 1)
                begin_x = 1 + direction * (shift_x - 1)
                window = padded[
                    :,
                    begin_z : begin_z + extent_z,
                    begin_y : begin_y + extent_y,
                    begin_x : begin_x + extent_x,
                ]
                summed = summed + filter_taps[:, tap_index][:, None, None, None] * window
    return summed


def lift(field_z):
    extended = field_z.astype(jnp.float32).reshape(field_z.shape[0], field_z.shape[1], CY, CX)
    return jnp.pad(extended, ((0, 0), (0, 0), (1, 1), (1, 1)))


def to_cells(field):
    return lax.all_to_all(
        field.reshape(field.shape[0], -1), "chan", split_axis=1, concat_axis=0, tiled=True
    )


def to_channels(field, slab_shape):
    return lax.all_to_all(field, "chan", split_axis=0, concat_axis=1, tiled=True).reshape(
        slab_shape
    )


def general_body(volume, out_grad, weight_in, weight_out, filter_taps, filter_bias):
    slab_shape = volume.shape
    contract_first = (((0,), (0,)), ((), ()))
    full_in, full_out = (
        lax.all_gather(weight_in, "chan", axis=0, tiled=True),
        lax.all_gather(weight_out, "chan", axis=0, tiled=True),
    )
    vol_cells = to_cells(volume)
    hidden = to_channels(
        jnp.dot(full_in, vol_cells, preferred_element_type=jnp.float32).astype(jnp.bfloat16),
        slab_shape,
    )
    padded = lift(with_halo(hidden, (("space", 1),), 1))
    mixed = core(padded, filter_taps, 1) + filter_bias[:, None, None, None]
    active = gelu_value(mixed).astype(jnp.bfloat16).reshape(slab_shape)
    act_cells = to_cells(active)
    out_cells = vol_cells.astype(jnp.float32) + jnp.dot(
        full_out, act_cells, preferred_element_type=jnp.float32
    )
    block_out = to_channels(out_cells.astype(jnp.bfloat16), slab_shape)
    grad_cells = to_cells(out_grad)
    act_part = lax.dot_general(
        full_out, grad_cells, contract_first, preferred_element_type=jnp.float32
    )
    act_grad = to_channels(act_part.astype(jnp.bfloat16), slab_shape)
    slope = gelu_slope(mixed)
    mix_grad = (
        (act_grad.astype(jnp.float32).reshape(slope.shape) * slope)
        .astype(jnp.bfloat16)
        .reshape(slab_shape)
    )
    padded_grad = lift(with_halo(mix_grad, (("space", 1),), 1))
    hid_grad = core(padded_grad, filter_taps, -1).astype(jnp.bfloat16).reshape(slab_shape)
    hid_cells = to_cells(hid_grad)
    back_part = lax.dot_general(
        full_in, hid_cells, contract_first, preferred_element_type=jnp.float32
    )
    volume_grad = to_channels(
        (grad_cells.astype(jnp.float32) + back_part).astype(jnp.bfloat16), slab_shape
    )
    return (block_out, volume_grad)


LANES = 128
TAP_ROWS = 32
MESH = pl.DeviceIdType.MESH
f32 = jnp.float32
bf16 = jnp.bfloat16


def rolled(value, shift):
    shift = shift % LANES
    return value if shift == 0 else pltpu.roll(value, shift, 1)


def kernel(
    nc,
    ns,
    vol,
    grd,
    win,
    wout,
    tap,
    bo,
    vg,
    cells,
    weights,
    tap_t,
    tap_s,
    field,
    pack_y,
    halo_y,
    pack_c,
    halo_c,
    active,
    slope,
    hid,
    stage,
    a_send,
    a_recv,
    w1_send,
    w1_recv,
    w2_send,
    w2_recv,
    t_send,
    t_recv,
    h_send,
    h_recv,
    own_sem,
):
    planes, block, _ = vol.shape
    channels = block * nc
    part = block // ns
    g = lax.axis_index("groups")
    c = lax.axis_index("chan")
    s = lax.axis_index("space")
    grads = (vol, grd)
    shards = (win, wout)
    outs = (bo, vg)

    def chan_peer(d):
        return lax.rem(c + d, nc)

    def space_peer(d):
        return lax.rem(s + d, ns)

    def rows_of(r):
        return pl.ds(pl.multiple_of(r * block, block), block)

    def lanes_of(q):
        return pl.ds(pl.multiple_of(q * LANES, LANES), LANES)

    def part_rows(r, q):
        return pl.ds(pl.multiple_of(r * block + q * part, part), part)

    def remote(src, dst, send, recv, to):
        return pltpu.make_async_remote_copy(
            src_ref=src, dst_ref=dst, send_sem=send, recv_sem=recv, device_id=to, device_id_type=MESH
        )

    def in_copy(k, frm, to):
        return remote(
            grads[k].at[:, :, lanes_of(to)],
            cells.at[k, :, rows_of(frm), :],
            a_send.at[k, to],
            a_recv.at[k, frm],
            (g, to, s),
        )

    def out_copy(k, frm, to):
        return remote(
            stage.at[k, :, rows_of(to), :],
            outs[k].at[:, :, lanes_of(frm)],
            a_send.at[2 + k, to],
            a_recv.at[2 + k, frm],
            (g, to, s),
        )

    def w1_copy(k, frm, to):
        return remote(
            shards[k].at[pl.ds(pl.multiple_of(s * part, part), part), :],
            weights.at[k, part_rows(frm, s), :],
            w1_send.at[k, to],
            w1_recv.at[k, frm],
            (g, to, s),
        )

    def w2_copy(k, shard, frm, to):
        return remote(
            weights.at[k, part_rows(shard, frm), :],
            weights.at[k, part_rows(shard, frm), :],
            w2_send.at[k, shard, to],
            w2_recv.at[k, shard, frm],
            (g, c, to),
        )

    def tap_copy(frm, to):
        return remote(tap, tap_t.at[frm], t_send.at[to], t_recv.at[frm], (g, to, s))

    def halo_copy(v, way, r):
        rw = rows_of(r)
        if way == 0:
            src, dst, to = pack_y.at[v, 0, rw, :], halo_y.at[v, 0, rw, :], (g, c + 1, s)
        elif way == 1:
            src, dst, to = pack_y.at[v, 1, rw, :], halo_y.at[v, 1, rw, :], (g, c - 1, s)
        elif way == 2:
            src, dst, to = field.at[v, planes, rw, :], field.at[v, 0, rw, :], (g, c, s + 1)
        elif way == 3:
            src, dst, to = field.at[v, 1, rw, :], field.at[v, planes + 1, rw, :], (g, c, s - 1)
        elif way == 4:
            src, dst, to = pack_c.at[v, 0, rw, :], halo_c.at[v, 0, rw, :], (g, c, s + 1)
        else:
            src, dst, to = pack_c.at[v, 1, rw, :], halo_c.at[v, 1, rw, :], (g, c, s - 1)
        return remote(src, dst, h_send.at[v, way, r], h_recv.at[v, way, r], to)

    sends_when = (c < nc - 1, c > 0, s < ns - 1, s > 0, s < ns - 1, s > 0)
    takes_when = (c > 0, c < nc - 1, s > 0, s < ns - 1, s > 0, s < ns - 1)

    def halo_start(v, ways, r):
        for way in ways:
            pl.when(sends_when[way])(lambda way=way: halo_copy(v, way, r).start())

    def halo_wait_recv(v, ways, r):
        for way in ways:
            pl.when(takes_when[way])(lambda way=way: halo_copy(v, way, r).wait_recv())

    def halo_wait_send(v, ways, r):
        for way in ways:
            pl.when(sends_when[way])(lambda way=way: halo_copy(v, way, r).wait_send())

    barrier = pltpu.get_barrier_semaphore()
    for d in range(1, nc):
        pl.semaphore_signal(barrier, inc=1, device_id=(g, chan_peer(d), s), device_id_type=MESH)
    for d in range(1, ns):
        pl.semaphore_signal(barrier, inc=1, device_id=(g, c, space_peer(d)), device_id_type=MESH)
    pl.semaphore_wait(barrier, nc + ns - 2)

    own = []
    for k in range(2):
        own.append(
            pltpu.make_async_copy(
                grads[k].at[:, :, lanes_of(c)], cells.at[k, :, rows_of(c), :], own_sem.at[2 * k]
            )
        )
        own.append(
            pltpu.make_async_copy(shards[k], weights.at[k, rows_of(c), :], own_sem.at[2 * k + 1])
        )

    for d in range(1, nc):
        w1_copy(0, c, chan_peer(d)).start()
    for d in range(1, nc):
        tap_copy(c, chan_peer(d)).start()
    for d in range(1, nc):
        in_copy(0, c, chan_peer(d)).start()
    for d in range(1, nc):
        w1_copy(1, c, chan_peer(d)).start()
    for d in range(1, nc):
        in_copy(1, c, chan_peer(d)).start()
    for copy in own:
        copy.start()

    zeros = jnp.zeros((channels, LANES), bf16)
    for v in range(2):

        @pl.when(c == 0)
        def _():
            halo_y[v, 0] = zeros

        @pl.when(c == nc - 1)
        def _():
            halo_y[v, 1] = zeros

        @pl.when(s == 0)
        def _():
            field[v, 0] = zeros
            halo_c[v, 0] = zeros

        @pl.when(s == ns - 1)
        def _():
            field[v, planes + 1] = zeros
            halo_c[v, 1] = zeros

    tap_t[c] = tap[...]

    def spread(k):
        for d in range(1, nc):
            p = chan_peer(d)
            w1_copy(k, p, c).wait_recv()
            for e in range(1, ns):
                w2_copy(k, p, s, space_peer(e)).start()

    def await_weights(k):
        for d in range(1, nc):
            p = chan_peer(d)
            for e in range(1, ns):
                w2_copy(k, p, space_peer(e), s).wait_recv()

    spread(0)
    for d in range(1, nc):
        tap_copy(chan_peer(d), c).wait_recv()
    for r in range(nc):
        tap_s[r * block : (r + 1) * block, 0:TAP_ROWS] = jnp.transpose(tap_t[r])
    for copy in own:
        copy.wait()
    for d in range(1, nc):
        in_copy(0, chan_peer(d), c).wait_recv()
    await_weights(0)

    def wide(ref, first, rw):
        return jnp.concatenate([ref[first + (z,) + (rw, slice(None))] for z in range(planes)], axis=1)

    every = slice(None)

    def pack(v, r):
        step = 32

        def one(i, carry):
            rw = pl.ds(pl.multiple_of(r * block + i * step, step), step)
            spot = lax.broadcasted_iota(jnp.int32, (step, LANES), 1)
            values = [field[v, 1 + z, rw, :].astype(f32) for z in range(planes)]
            high, low = values[planes - 1], values[0]
            high = rolled(values[planes - 1], CX * planes)
            for z in range(planes):
                here = (spot >= z * CX) & (spot < (z + 1) * CX)
                high = jnp.where(here, rolled(values[z], CX * (z + 1)), high)
                low = jnp.where(here, rolled(values[z], CX * z), low)
            pack_y[v, 0, rw, :] = high.astype(bf16)
            pack_y[v, 1, rw, :] = low.astype(bf16)
            return carry

        lax.fori_loop(0, block // step, one, 0)

    def corner(v, r):
        step = 32

        def one(i, carry):
            rw = pl.ds(pl.multiple_of(r * block + i * step, step), step)
            spot = lax.broadcasted_iota(jnp.int32, (step, LANES), 1)
            low = halo_y[v, 0, rw, :].astype(f32)
            high = halo_y[v, 1, rw, :].astype(f32)
            last = LANES - CX
            first = spot < CX
            z = planes - 1
            pack_c[v, 0, rw, :] = jnp.where(first, rolled(low, -CX * z), rolled(high, last - CX * z)).astype(bf16)
            pack_c[v, 1, rw, :] = jnp.where(first, low, rolled(high, last)).astype(bf16)
            return carry

        lax.fori_loop(0, block // step, one, 0)

    def convolve(v, r, finish):
        step = 16
        half = 8

        def one(i, carry):
            rw = pl.ds(pl.multiple_of(r * block + i * step, step), step)
            spot = lax.broadcasted_iota(jnp.int32, (half, LANES), 1)
            column = lax.rem(spot, CX)
            first = spot < CX
            final = spot >= LANES - CX
            loaded = [field[v, z, rw, :].astype(f32) for z in range(planes + 2)]
            low = halo_y[v, 0, rw, :].astype(f32)
            high = halo_y[v, 1, rw, :].astype(f32)
            below = halo_c[v, 0, rw, :].astype(f32)
            above = halo_c[v, 1, rw, :].astype(f32)
            taps = tap_s[rw, :]
            results = [[] for _ in range(planes)]
            for q in range(step // half):
                cut = slice(q * half, (q + 1) * half)
                shifted = []
                for z in range(planes + 2):
                    value = loaded[z][cut]
                    if z == 0:
                        under = over = below[cut]
                    elif z == planes + 1:
                        under = over = above[cut]
                    else:
                        under = rolled(low[cut], -CX * (z - 1))
                        over = rolled(high[cut], LANES - CX - CX * (z - 1))
                    shifted.append(
                        (
                            jnp.where(first, under, rolled(value, CX)),
                            value,
                            jnp.where(final, over, rolled(value, -CX)),
                        )
                    )
                weight = []
                for k in range(27):
                    at = k if v == 0 else 26 - k
                    weight.append(jnp.broadcast_to(taps[cut, at : at + 1], (half, LANES)))
                bias = jnp.broadcast_to(taps[cut, 27:28], (half, LANES)) if v == 0 else None
                for z in range(planes):
                    sums = [None, None, None]
                    for a in range(3):
                        for b in range(3):
                            for e in range(3):
                                term = weight[9 * a + 3 * b + e] * shifted[z + a][b]
                                sums[e] = term if sums[e] is None else sums[e] + term
                    total = sums[1]
                    total = total + jnp.where(column == 0, 0.0, rolled(sums[0], 1))
                    total = total + jnp.where(column == CX - 1, 0.0, rolled(sums[2], -1))
                    if bias is not None:
                        total = total + bias
                    results[z].append(total)
            for z in range(planes):
                finish(z, rw, jnp.concatenate(results[z], axis=0))
            return carry

        lax.fori_loop(0, block // step, one, 0)

    def finish_forward(z, rw, mixed):
        up = 0.5 * (1.0 + lax.erf(mixed * root_half))
        active[z, rw, :] = (mixed * up).astype(bf16)
        slope[z, rw, :] = up + mixed * jnp.exp(-0.5 * mixed * mixed) * inv_root_two_pi

    def finish_backward(z, rw, total):
        hid[z, rw, :] = total.astype(bf16)

    def hidden_chunk(r, carry):
        rw = rows_of(r)
        value = jnp.dot(weights[0, rw, :], wide(cells, (0,), every), preferred_element_type=f32)
        for z in range(planes):
            field[0, 1 + z, rw, :] = value[:, z * LANES : (z + 1) * LANES].astype(bf16)
        halo_start(0, (2, 3), r)
        pack(0, r)
        halo_start(0, (0, 1), r)
        return carry

    def corner_chunk(v):
        def run(r, carry):
            halo_wait_recv(v, (0, 1), r)
            corner(v, r)
            halo_start(v, (4, 5), r)
            return carry

        lax.fori_loop(0, nc, run, 0)

    def conv_chunk(v, finish):
        def run(r, carry):
            halo_wait_recv(v, (2, 3, 4, 5), r)
            convolve(v, r, finish)
            return carry

        lax.fori_loop(0, nc, run, 0)

    def out_chunk(k, r, value):
        total = wide(cells, (k,), rows_of(r)).astype(f32) + value
        for z in range(planes):
            stage[k, z, rows_of(r), :] = total[:, z * LANES : (z + 1) * LANES].astype(bf16)

        @pl.when(r != c)
        def _():
            out_copy(k, c, r).start()

        @pl.when(r == c)
        def _():
            outs[k][:, :, lanes_of(c)] = stage[k, :, rows_of(r), :]

    def block_chunk(r, carry):
        value = jnp.dot(weights[1, rows_of(r), :], wide(active, (), every), preferred_element_type=f32)
        out_chunk(0, r, value)
        return carry

    def flipped(k, r, right):
        return lax.dot_general(
            weights[k, :, rows_of(r)], right, (((0,), (0,)), ((), ())), preferred_element_type=f32
        )

    def mix_chunk(r, carry):
        rw = rows_of(r)
        value = flipped(1, r, wide(cells, (1,), every))
        for z in range(planes):
            act = value[:, z * LANES : (z + 1) * LANES].astype(bf16).astype(f32)
            field[1, 1 + z, rw, :] = (act * slope[z, rw, :]).astype(bf16)
        halo_start(1, (2, 3), r)
        pack(1, r)
        halo_start(1, (0, 1), r)
        return carry

    def back_chunk(r, carry):
        out_chunk(1, r, flipped(0, r, wide(hid, (), every)))
        return carry

    lax.fori_loop(0, nc, hidden_chunk, 0)
    spread(1)
    corner_chunk(0)
    conv_chunk(0, finish_forward)
    await_weights(1)
    lax.fori_loop(0, nc, block_chunk, 0)
    for d in range(1, nc):
        in_copy(1, chan_peer(d), c).wait_recv()
    lax.fori_loop(0, nc, mix_chunk, 0)
    corner_chunk(1)
    conv_chunk(1, finish_backward)
    lax.fori_loop(0, nc, back_chunk, 0)

    for d in range(1, nc):
        p = chan_peer(d)
        tap_copy(c, p).wait_send()
        for k in range(2):
            w1_copy(k, c, p).wait_send()
            in_copy(k, c, p).wait_send()
            for e in range(1, ns):
                w2_copy(k, p, s, space_peer(e)).wait_send()

    def drain(r, carry):
        for v in range(2):
            halo_wait_send(v, range(6), r)
        return carry

    lax.fori_loop(0, nc, drain, 0)
    for d in range(1, nc):
        p = chan_peer(d)
        for k in range(2):
            out_copy(k, c, p).wait_send()
            out_copy(k, p, c).wait_recv()


def body(mesh, volume, out_grad, weight_in, weight_out, filter_taps, filter_bias):
    nc, ns = mesh.shape["chan"], mesh.shape["space"]
    block, planes, plane = volume.shape
    channels = weight_in.shape[1]
    fits = (
        nc > 1
        and ns > 1
        and plane == nc * LANES
        and plane == CX * CY
        and planes * CX == LANES
        and block * nc == channels
        and block % (ns * 16) == 0
        and block % LANES == 0
    )
    if not fits:
        return general_body(volume, out_grad, weight_in, weight_out, filter_taps, filter_bias)
    spare = jnp.zeros((TAP_ROWS - filter_taps.shape[1] - 1, block), f32)
    tap = jnp.concatenate([filter_taps.T, filter_bias[None, :], spare], axis=0)
    shape = jax.ShapeDtypeStruct((planes, block, plane), bf16)
    vmem = pl.BlockSpec(memory_space=pltpu.VMEM)
    dma = pltpu.SemaphoreType.DMA
    block_out, volume_grad = pl.pallas_call(
        functools.partial(kernel, nc, ns),
        out_shape=(shape, shape),
        in_specs=[vmem] * 5,
        out_specs=(vmem, vmem),
        scratch_shapes=[
            pltpu.VMEM((2, planes, channels, LANES), bf16),
            pltpu.VMEM((2, channels, channels), bf16),
            pltpu.VMEM((nc, TAP_ROWS, block), f32),
            pltpu.VMEM((channels, LANES), f32),
            pltpu.VMEM((2, planes + 2, channels, LANES), bf16),
            pltpu.VMEM((2, 2, channels, LANES), bf16),
            pltpu.VMEM((2, 2, channels, LANES), bf16),
            pltpu.VMEM((2, 2, channels, LANES), bf16),
            pltpu.VMEM((2, 2, channels, LANES), bf16),
            pltpu.VMEM((planes, channels, LANES), bf16),
            pltpu.VMEM((planes, channels, LANES), f32),
            pltpu.VMEM((planes, channels, LANES), bf16),
            pltpu.VMEM((2, planes, channels, LANES), bf16),
            dma((4, nc)),
            dma((4, nc)),
            dma((2, nc)),
            dma((2, nc)),
            dma((2, nc, ns)),
            dma((2, nc, ns)),
            dma((nc,)),
            dma((nc,)),
            dma((2, 6, nc)),
            dma((2, 6, nc)),
            dma((4,)),
        ],
        compiler_params=pltpu.CompilerParams(
            collective_id=0, has_side_effects=True, vmem_limit_bytes=56 * 1024 * 1024
        ),
        cost_estimate=pl.CostEstimate(
            flops=8 * channels * channels * plane, bytes_accessed=12 * block * plane * planes, transcendentals=0
        ),
    )(
        jnp.transpose(volume, (1, 0, 2)),
        jnp.transpose(out_grad, (1, 0, 2)),
        weight_in,
        weight_out,
        tap,
    )
    return jnp.transpose(block_out, (1, 0, 2)), jnp.transpose(volume_grad, (1, 0, 2))


def solution(mesh):
    placed = (
        P(("groups", "chan"), "space", None),
        P(("groups", "chan"), "space", None),
        P("chan", None),
        P("chan", None),
        P("chan", None),
        P("chan"),
    )
    return jax.shard_map(
        functools.partial(body, mesh),
        mesh=mesh,
        in_specs=placed,
        out_specs=(P(("groups", "chan"), "space", None), P(("groups", "chan"), "space", None)),
        check_vma=False,
    )
```

```python
import functools

import jax
import jax.numpy as jnp
from jax import lax
from jax.experimental import pallas as pl
from jax.experimental.pallas import tpu as pltpu
from jax.sharding import PartitionSpec as P

CX = 32
CY = 16


root_half = 0.7071067811865476
inv_root_two_pi = 0.3989422804014327


def with_halo(block, sides, width):
    for axis, dim in sides:
        count = lax.axis_size(axis)
        forward = [(i, i + 1) for i in range(count - 1)]
        backward = [(target, source) for source, target in forward]
        low = lax.ppermute(
            lax.slice_in_dim(block, block.shape[dim] - width, None, axis=dim), axis, forward
        )
        high = lax.ppermute(lax.slice_in_dim(block, 0, width, axis=dim), axis, backward)
        block = jnp.concatenate([low, block, high], axis=dim)
    return block


def gelu_value(field):
    return 0.5 * field * (1.0 + lax.erf(field * root_half))


def gelu_slope(field):
    return (
        0.5 * (1.0 + lax.erf(field * root_half))
        + field * jnp.exp(-0.5 * field * field) * inv_root_two_pi
    )


def core(padded, filter_taps, direction):
    extent_z = padded.shape[1] - 2
    extent_y = padded.shape[2] - 2
    extent_x = padded.shape[3] - 2
    summed = jnp.zeros((padded.shape[0], extent_z, extent_y, extent_x), jnp.float32)
    for shift_z in range(3):
        for shift_y in range(3):
            for shift_x in range(3):
                tap_index = (shift_z * 3 + shift_y) * 3 + shift_x
                begin_z = 1 + direction * (shift_z - 1)
                begin_y = 1 + direction * (shift_y - 1)
                begin_x = 1 + direction * (shift_x - 1)
                window = padded[
                    :,
                    begin_z : begin_z + extent_z,
                    begin_y : begin_y + extent_y,
                    begin_x : begin_x + extent_x,
                ]
                summed = summed + filter_taps[:, tap_index][:, None, None, None] * window
    return summed


def lift(field_z):
    extended = field_z.astype(jnp.float32).reshape(field_z.shape[0], field_z.shape[1], CY, CX)
    return jnp.pad(extended, ((0, 0), (0, 0), (1, 1), (1, 1)))


def to_cells(field):
    return lax.all_to_all(
        field.reshape(field.shape[0], -1), "chan", split_axis=1, concat_axis=0, tiled=True
    )


def to_channels(field, slab_shape):
    return lax.all_to_all(field, "chan", split_axis=0, concat_axis=1, tiled=True).reshape(
        slab_shape
    )


def general_body(volume, out_grad, weight_in, weight_out, filter_taps, filter_bias):
    slab_shape = volume.shape
    contract_first = (((0,), (0,)), ((), ()))
    full_in, full_out = (
        lax.all_gather(weight_in, "chan", axis=0, tiled=True),
        lax.all_gather(weight_out, "chan", axis=0, tiled=True),
    )
    vol_cells = to_cells(volume)
    hidden = to_channels(
        jnp.dot(full_in, vol_cells, preferred_element_type=jnp.float32).astype(jnp.bfloat16),
        slab_shape,
    )
    padded = lift(with_halo(hidden, (("space", 1),), 1))
    mixed = core(padded, filter_taps, 1) + filter_bias[:, None, None, None]
    active = gelu_value(mixed).astype(jnp.bfloat16).reshape(slab_shape)
    act_cells = to_cells(active)
    out_cells = vol_cells.astype(jnp.float32) + jnp.dot(
        full_out, act_cells, preferred_element_type=jnp.float32
    )
    block_out = to_channels(out_cells.astype(jnp.bfloat16), slab_shape)
    grad_cells = to_cells(out_grad)
    act_part = lax.dot_general(
        full_out, grad_cells, contract_first, preferred_element_type=jnp.float32
    )
    act_grad = to_channels(act_part.astype(jnp.bfloat16), slab_shape)
    slope = gelu_slope(mixed)
    mix_grad = (
        (act_grad.astype(jnp.float32).reshape(slope.shape) * slope)
        .astype(jnp.bfloat16)
        .reshape(slab_shape)
    )
    padded_grad = lift(with_halo(mix_grad, (("space", 1),), 1))
    hid_grad = core(padded_grad, filter_taps, -1).astype(jnp.bfloat16).reshape(slab_shape)
    hid_cells = to_cells(hid_grad)
    back_part = lax.dot_general(
        full_in, hid_cells, contract_first, preferred_element_type=jnp.float32
    )
    volume_grad = to_channels(
        (grad_cells.astype(jnp.float32) + back_part).astype(jnp.bfloat16), slab_shape
    )
    return (block_out, volume_grad)


LANES = 128
TAP_ROWS = 32
MESH = pl.DeviceIdType.MESH
f32 = jnp.float32
bf16 = jnp.bfloat16


def rolled(value, shift):
    shift = shift % LANES
    return value if shift == 0 else pltpu.roll(value, shift, 1)


def kernel(
    nc,
    ns,
    vol,
    grd,
    win,
    wout,
    tap,
    bo,
    vg,
    cells,
    weights,
    tap_t,
    tap_s,
    field,
    pack_y,
    halo_y,
    pack_c,
    halo_c,
    active,
    slope,
    hid,
    stage,
    a_send,
    a_recv,
    w1_send,
    w1_recv,
    w2_send,
    w2_recv,
    t_send,
    t_recv,
    h_send,
    h_recv,
    own_sem,
):
    planes, block, _ = vol.shape
    channels = block * nc
    part = block // ns
    g = lax.axis_index("groups")
    c = lax.axis_index("chan")
    s = lax.axis_index("space")
    grads = (vol, grd)
    shards = (win, wout)
    outs = (bo, vg)

    def chan_peer(d):
        return lax.rem(c + d, nc)

    def space_peer(d):
        return lax.rem(s + d, ns)

    def rows_of(r):
        return pl.ds(pl.multiple_of(r * block, block), block)

    def lanes_of(q):
        return pl.ds(pl.multiple_of(q * LANES, LANES), LANES)

    def part_rows(r, q):
        return pl.ds(pl.multiple_of(r * block + q * part, part), part)

    def remote(src, dst, send, recv, to):
        return pltpu.make_async_remote_copy(
            src_ref=src, dst_ref=dst, send_sem=send, recv_sem=recv, device_id=to, device_id_type=MESH
        )

    def in_copy(k, frm, to):
        return remote(
            grads[k].at[:, :, lanes_of(to)],
            cells.at[k, :, rows_of(frm), :],
            a_send.at[k, to],
            a_recv.at[k, frm],
            (g, to, s),
        )

    def out_copy(k, frm, to):
        return remote(
            stage.at[k, :, rows_of(to), :],
            outs[k].at[:, :, lanes_of(frm)],
            a_send.at[2 + k, to],
            a_recv.at[2 + k, frm],
            (g, to, s),
        )

    def w1_copy(k, frm, to):
        return remote(
            shards[k].at[pl.ds(pl.multiple_of(s * part, part), part), :],
            weights.at[k, part_rows(frm, s), :],
            w1_send.at[k, to],
            w1_recv.at[k, frm],
            (g, to, s),
        )

    across = lax.rem(s + ns // 2, ns)
    sibling = s + 1 - 2 * lax.rem(s, 2)
    sibling_across = lax.rem(sibling + ns // 2, ns)

    def w2_copy(k, shard, hop, sending):
        held = ((s, across), (s, sibling), (across, sibling_across))[hop][0 if sending else 1]
        rw = part_rows(shard, held)
        return remote(
            weights.at[k, rw, :],
            weights.at[k, rw, :],
            w2_send.at[k, shard, hop],
            w2_recv.at[k, shard, hop],
            (g, c, across if hop == 0 else sibling),
        )

    def tap_copy(frm, to):
        return remote(tap, tap_t.at[frm], t_send.at[to], t_recv.at[frm], (g, to, s))

    def halo_copy(v, way, r):
        rw = rows_of(r)
        if way == 0:
            src, dst, to = pack_y.at[v, 0, rw, :], halo_y.at[v, 0, rw, :], (g, c + 1, s)
        elif way == 1:
            src, dst, to = pack_y.at[v, 1, rw, :], halo_y.at[v, 1, rw, :], (g, c - 1, s)
        elif way == 2:
            src, dst, to = field.at[v, planes, rw, :], field.at[v, 0, rw, :], (g, c, s + 1)
        elif way == 3:
            src, dst, to = field.at[v, 1, rw, :], field.at[v, planes + 1, rw, :], (g, c, s - 1)
        elif way == 4:
            src, dst, to = pack_c.at[v, 0, rw, :], halo_c.at[v, 0, rw, :], (g, c, s + 1)
        else:
            src, dst, to = pack_c.at[v, 1, rw, :], halo_c.at[v, 1, rw, :], (g, c, s - 1)
        return remote(src, dst, h_send.at[v, way, r], h_recv.at[v, way, r], to)

    sends_when = (c < nc - 1, c > 0, s < ns - 1, s > 0, s < ns - 1, s > 0)
    takes_when = (c > 0, c < nc - 1, s > 0, s < ns - 1, s > 0, s < ns - 1)

    def halo_start(v, ways, r):
        for way in ways:
            pl.when(sends_when[way])(lambda way=way: halo_copy(v, way, r).start())

    def halo_wait_recv(v, ways, r):
        for way in ways:
            pl.when(takes_when[way])(lambda way=way: halo_copy(v, way, r).wait_recv())

    def halo_wait_send(v, ways, r):
        for way in ways:
            pl.when(sends_when[way])(lambda way=way: halo_copy(v, way, r).wait_send())

    barrier = pltpu.get_barrier_semaphore()
    for d in range(1, nc):
        pl.semaphore_signal(barrier, inc=1, device_id=(g, chan_peer(d), s), device_id_type=MESH)
    for d in range(1, ns):
        pl.semaphore_signal(barrier, inc=1, device_id=(g, c, space_peer(d)), device_id_type=MESH)
    pl.semaphore_wait(barrier, nc + ns - 2)

    own = []
    for k in range(2):
        own.append(
            pltpu.make_async_copy(
                grads[k].at[:, :, lanes_of(c)], cells.at[k, :, rows_of(c), :], own_sem.at[2 * k]
            )
        )
        own.append(
            pltpu.make_async_copy(shards[k], weights.at[k, rows_of(c), :], own_sem.at[2 * k + 1])
        )

    for d in range(1, nc):
        w1_copy(0, c, chan_peer(d)).start()
    for d in range(1, nc):
        tap_copy(c, chan_peer(d)).start()
    for d in range(1, nc):
        in_copy(0, c, chan_peer(d)).start()
    for d in range(1, nc):
        w1_copy(1, c, chan_peer(d)).start()
    for copy in own:
        copy.start()

    zeros = jnp.zeros((channels, LANES), bf16)
    for v in range(2):

        @pl.when(c == 0)
        def _():
            halo_y[v, 0] = zeros

        @pl.when(c == nc - 1)
        def _():
            halo_y[v, 1] = zeros

        @pl.when(s == 0)
        def _():
            field[v, 0] = zeros
            halo_c[v, 0] = zeros

        @pl.when(s == ns - 1)
        def _():
            field[v, planes + 1] = zeros
            halo_c[v, 1] = zeros

    tap_t[c] = tap[...]

    def spread(k):
        for d in range(1, nc):
            p = chan_peer(d)
            w1_copy(k, p, c).wait_recv()
            w2_copy(k, p, 0, True).start()
            w2_copy(k, p, 1, True).start()

    def hand_on(k):
        for d in range(1, nc):
            p = chan_peer(d)
            w2_copy(k, p, 0, False).wait_recv()
            w2_copy(k, p, 2, True).start()

    def await_weights(k):
        for d in range(1, nc):
            for hop in (1, 2):
                w2_copy(k, chan_peer(d), hop, False).wait_recv()

    spread(0)
    for d in range(1, nc):
        tap_copy(chan_peer(d), c).wait_recv()
    for r in range(nc):
        columns = jnp.transpose(tap_t[r])
        for k in range(28):
            tap_s[k, r * block : (r + 1) * block, :] = jnp.broadcast_to(columns[:, k : k + 1], (block, LANES))
    hand_on(0)
    for copy in own:
        copy.wait()
    for d in range(1, nc):
        in_copy(0, chan_peer(d), c).wait_recv()
    await_weights(0)

    def wide(ref, first, rw):
        return jnp.concatenate([ref[first + (z,) + (rw, slice(None))] for z in range(planes)], axis=1)

    every = slice(None)

    def pack(v, r):
        step = 32

        def one(i, carry):
            rw = pl.ds(pl.multiple_of(r * block + i * step, step), step)
            spot = lax.broadcasted_iota(jnp.int32, (step, LANES), 1)
            values = [field[v, 1 + z, rw, :].astype(f32) for z in range(planes)]
            high, low = values[planes - 1], values[0]
            high = rolled(values[planes - 1], CX * planes)
            for z in range(planes):
                here = (spot >= z * CX) & (spot < (z + 1) * CX)
                high = jnp.where(here, rolled(values[z], CX * (z + 1)), high)
                low = jnp.where(here, rolled(values[z], CX * z), low)
            pack_y[v, 0, rw, :] = high.astype(bf16)
            pack_y[v, 1, rw, :] = low.astype(bf16)
            return carry

        lax.fori_loop(0, block // step, one, 0, unroll=True)

    def corner(v, r):
        step = 32

        def one(i, carry):
            rw = pl.ds(pl.multiple_of(r * block + i * step, step), step)
            spot = lax.broadcasted_iota(jnp.int32, (step, LANES), 1)
            low = halo_y[v, 0, rw, :].astype(f32)
            high = halo_y[v, 1, rw, :].astype(f32)
            last = LANES - CX
            first = spot < CX
            z = planes - 1
            pack_c[v, 0, rw, :] = jnp.where(first, rolled(low, -CX * z), rolled(high, last - CX * z)).astype(bf16)
            pack_c[v, 1, rw, :] = jnp.where(first, low, rolled(high, last)).astype(bf16)
            return carry

        lax.fori_loop(0, block // step, one, 0, unroll=True)

    def convolve(v, r, finish):
        step = 16
        half = 8

        def one(i, carry):
            rw = pl.ds(pl.multiple_of(r * block + i * step, step), step)
            spot = lax.broadcasted_iota(jnp.int32, (half, LANES), 1)
            column = lax.rem(spot, CX)
            first = spot < CX
            final = spot >= LANES - CX
            loaded = [field[v, z, rw, :].astype(f32) for z in range(planes + 2)]
            low = halo_y[v, 0, rw, :].astype(f32)
            high = halo_y[v, 1, rw, :].astype(f32)
            below = halo_c[v, 0, rw, :].astype(f32)
            above = halo_c[v, 1, rw, :].astype(f32)
            results = [[] for _ in range(planes)]
            for q in range(step // half):
                cut = slice(q * half, (q + 1) * half)
                shifted = []
                for z in range(planes + 2):
                    value = loaded[z][cut]
                    if z == 0:
                        under = over = below[cut]
                    elif z == planes + 1:
                        under = over = above[cut]
                    else:
                        under = rolled(low[cut], -CX * (z - 1))
                        over = rolled(high[cut], LANES - CX - CX * (z - 1))
                    shifted.append(
                        (
                            jnp.where(first, under, rolled(value, CX)),
                            value,
                            jnp.where(final, over, rolled(value, -CX)),
                        )
                    )
                weight = []
                for k in range(27):
                    at = k if v == 0 else 26 - k
                    weight.append(tap_s[at, pl.ds(pl.multiple_of(r * block + i * step + q * half, half), half), :])
                bias = tap_s[27, pl.ds(pl.multiple_of(r * block + i * step + q * half, half), half), :] if v == 0 else None
                for z in range(planes):
                    sums = [None, None, None]
                    for a in range(3):
                        for b in range(3):
                            for e in range(3):
                                term = weight[9 * a + 3 * b + e] * shifted[z + a][b]
                                sums[e] = term if sums[e] is None else sums[e] + term
                    total = sums[1]
                    total = total + jnp.where(column == 0, 0.0, rolled(sums[0], 1))
                    total = total + jnp.where(column == CX - 1, 0.0, rolled(sums[2], -1))
                    if bias is not None:
                        total = total + bias
                    results[z].append(total)
            for z in range(planes):
                finish(z, rw, jnp.concatenate(results[z], axis=0))
            return carry

        lax.fori_loop(0, block // step, one, 0, unroll=4)

    def finish_forward(z, rw, mixed):
        up = 0.5 * (1.0 + lax.erf(mixed * root_half))
        active[z, rw, :] = (mixed * up).astype(bf16)
        slope[z, rw, :] = up + mixed * jnp.exp(-0.5 * mixed * mixed) * inv_root_two_pi

    def finish_backward(z, rw, total):
        hid[z, rw, :] = total.astype(bf16)

    def hidden_chunk(r, carry):
        rw = rows_of(r)
        value = jnp.dot(weights[0, rw, :], wide(cells, (0,), every), preferred_element_type=f32)
        for z in range(planes):
            field[0, 1 + z, rw, :] = value[:, z * LANES : (z + 1) * LANES].astype(bf16)
        halo_start(0, (2, 3), r)
        pack(0, r)
        halo_start(0, (0, 1), r)
        return carry

    def corner_chunk(v):
        def run(r, carry):
            halo_wait_recv(v, (0, 1), r)
            corner(v, r)
            halo_start(v, (4, 5), r)
            return carry

        lax.fori_loop(0, nc, run, 0)

    def conv_chunk(v, finish, begin, end):
        def run(r, carry):
            halo_wait_recv(v, (2, 3, 4, 5), r)
            convolve(v, r, finish)
            return carry

        lax.fori_loop(begin, end, run, 0)

    def out_chunk(k, r, value):
        total = wide(cells, (k,), rows_of(r)).astype(f32) + value
        for z in range(planes):
            stage[k, z, rows_of(r), :] = total[:, z * LANES : (z + 1) * LANES].astype(bf16)

    def out_start(k, r):
        @pl.when(r != c)
        def _():
            out_copy(k, c, r).start()

        @pl.when(r == c)
        def _():
            outs[k][:, :, lanes_of(c)] = stage[k, :, rows_of(r), :]

    def block_chunk(r, carry):
        value = jnp.dot(weights[1, rows_of(r), :], wide(active, (), every), preferred_element_type=f32)
        out_chunk(0, r, value)
        return carry

    def flipped(k, r, right):
        return lax.dot_general(
            weights[k, :, rows_of(r)], right, (((0,), (0,)), ((), ())), preferred_element_type=f32
        )

    def mix_chunk(r, carry):
        rw = rows_of(r)
        value = flipped(1, r, wide(cells, (1,), every))
        for z in range(planes):
            act = value[:, z * LANES : (z + 1) * LANES].astype(bf16).astype(f32)
            field[1, 1 + z, rw, :] = (act * slope[z, rw, :]).astype(bf16)
        halo_start(1, (2, 3), r)
        pack(1, r)
        halo_start(1, (0, 1), r)
        return carry

    def back_chunk(r, carry):
        out_chunk(1, r, flipped(0, r, wide(hid, (), every)))
        out_start(1, r)
        return carry

    def send_block(r, carry):
        out_start(0, r)
        return carry

    lax.fori_loop(0, nc, hidden_chunk, 0)
    for d in range(1, nc):
        in_copy(1, c, chan_peer(d)).start()
    corner_chunk(0)
    spread(1)
    conv_chunk(0, finish_forward, 0, nc // 2)
    hand_on(1)
    conv_chunk(0, finish_forward, nc // 2, nc)
    await_weights(1)
    lax.fori_loop(0, nc, block_chunk, 0)
    for d in range(1, nc):
        in_copy(1, chan_peer(d), c).wait_recv()
    lax.fori_loop(0, nc, mix_chunk, 0)
    lax.fori_loop(0, nc, send_block, 0)
    corner_chunk(1)
    conv_chunk(1, finish_backward, 0, nc)
    lax.fori_loop(0, nc, back_chunk, 0)

    for d in range(1, nc):
        p = chan_peer(d)
        tap_copy(c, p).wait_send()
        for k in range(2):
            w1_copy(k, c, p).wait_send()
            in_copy(k, c, p).wait_send()
            for hop in range(3):
                w2_copy(k, p, hop, True).wait_send()

    def drain(r, carry):
        for v in range(2):
            halo_wait_send(v, range(6), r)
        return carry

    lax.fori_loop(0, nc, drain, 0)
    for d in range(1, nc):
        p = chan_peer(d)
        for k in range(2):
            out_copy(k, c, p).wait_send()
            out_copy(k, p, c).wait_recv()


def body(mesh, volume, out_grad, weight_in, weight_out, filter_taps, filter_bias):
    nc, ns = mesh.shape["chan"], mesh.shape["space"]
    block, planes, plane = volume.shape
    channels = weight_in.shape[1]
    fits = (
        nc > 1
        and ns == 4
        and plane == nc * LANES
        and plane == CX * CY
        and planes * CX == LANES
        and block * nc == channels
        and block % (ns * 16) == 0
        and block % LANES == 0
    )
    if not fits:
        return general_body(volume, out_grad, weight_in, weight_out, filter_taps, filter_bias)
    spare = jnp.zeros((TAP_ROWS - filter_taps.shape[1] - 1, block), f32)
    tap = jnp.concatenate([filter_taps.T, filter_bias[None, :], spare], axis=0)
    shape = jax.ShapeDtypeStruct((planes, block, plane), bf16)
    vmem = pl.BlockSpec(memory_space=pltpu.VMEM)
    dma = pltpu.SemaphoreType.DMA
    block_out, volume_grad = pl.pallas_call(
        functools.partial(kernel, nc, ns),
        out_shape=(shape, shape),
        in_specs=[vmem] * 5,
        out_specs=(vmem, vmem),
        scratch_shapes=[
            pltpu.VMEM((2, planes, channels, LANES), bf16),
            pltpu.VMEM((2, channels, channels), bf16),
            pltpu.VMEM((nc, TAP_ROWS, block), f32),
            pltpu.VMEM((28, channels, LANES), f32),
            pltpu.VMEM((2, planes + 2, channels, LANES), bf16),
            pltpu.VMEM((2, 2, channels, LANES), bf16),
            pltpu.VMEM((2, 2, channels, LANES), bf16),
            pltpu.VMEM((2, 2, channels, LANES), bf16),
            pltpu.VMEM((2, 2, channels, LANES), bf16),
            pltpu.VMEM((planes, channels, LANES), bf16),
            pltpu.VMEM((planes, channels, LANES), f32),
            pltpu.VMEM((planes, channels, LANES), bf16),
            pltpu.VMEM((2, planes, channels, LANES), bf16),
            dma((4, nc)),
            dma((4, nc)),
            dma((2, nc)),
            dma((2, nc)),
            dma((2, nc, 3)),
            dma((2, nc, 3)),
            dma((nc,)),
            dma((nc,)),
            dma((2, 6, nc)),
            dma((2, 6, nc)),
            dma((4,)),
        ],
        compiler_params=pltpu.CompilerParams(
            collective_id=0, has_side_effects=True, vmem_limit_bytes=56 * 1024 * 1024
        ),
        cost_estimate=pl.CostEstimate(
            flops=8 * channels * channels * plane, bytes_accessed=12 * block * plane * planes, transcendentals=0
        ),
    )(
        jnp.transpose(volume, (1, 0, 2)),
        jnp.transpose(out_grad, (1, 0, 2)),
        weight_in,
        weight_out,
        tap,
    )
    return jnp.transpose(block_out, (1, 0, 2)), jnp.transpose(volume_grad, (1, 0, 2))


def solution(mesh):
    placed = (
        P(("groups", "chan"), "space", None),
        P(("groups", "chan"), "space", None),
        P("chan", None),
        P("chan", None),
        P("chan", None),
        P("chan"),
    )
    return jax.shard_map(
        functools.partial(body, mesh),
        mesh=mesh,
        in_specs=placed,
        out_specs=(P(("groups", "chan"), "space", None), P(("groups", "chan"), "space", None)),
        check_vma=False,
    )
```
